32 devices in a mesh: region: 8 (over y, x, core), local: 4 (over z).
Axes of the slice: x: 2, y: 2, z: 4, core: 2. Of those that a mesh axis runs over, the one named last changes fastest.
Arguments:
- tokens: bfloat16 [1024, 7168], P('region', 'local'), may hold values from -44 to 44
- norm_gain: float32 [7168], P('local'), may hold values from 0.1 to 1.9
- w_gate: bfloat16 [8, 7168, 2048], P('region', None, 'local'), may hold values from -0.0625 to 0.0625
- w_up: bfloat16 [8, 7168, 2048], P('region', None, 'local'), may hold values from -0.0625 to 0.0625
- w_down: bfloat16 [8, 2048, 7168], P('region', 'local'), may hold values from -0.125 to 0.125
- regions: int32 [1024, 2], P('region'), may hold values from 0 to 7, all different within a row; in each aligned block of 128 rows (0 to 127, 128 to 255, ...) at most 40 rows name the same one
- combine: float32 [1024, 2], P('region'), may hold values from 0.1 to 1
- grad_out: bfloat16 [1024, 7168], P('region', 'local'), may hold values from -3 to 3
Outputs:
- moe_out: bfloat16 [1024, 7168], P('region', 'local')
- grad_tokens: bfloat16 [1024, 7168], P('region', 'local')
- grad_combine: float32 [1024, 2], P('region')
The draws below stay inside these ranges and needn't reach their ends.
Inputs may be any that keep to these rules, and one draw needn't show every extreme that they name: `regions`: each row names 2 different experts; among the rows of one device (aligned blocks of 128 rows) no expert is named by more than 40 rows, a bound that some block reaches.
All inputs are finite; a program needn't handle non-finite values.
Results may differ from the reference program's by a relative error of at most 0.02.
Values may be sent and summed in bfloat16 or wider, within the bound.
A program may use at most 128 MiB of HBM per device.

```python
import math
import jax
import jax.numpy as jnp
import numpy as np
from jax import lax

D = 7168
HID = 2048
TOP = 2
T_DEV = 128
TOKENS = 1024
EXPERTS = 8
CAP = 40
N_REGION = 8


def draw_tokens(key, part):
    key_base, key_cols, key_rows = jax.random.split(key, 3)
    position = jnp.arange(D, dtype=jnp.float32) / D
    roughness = jnp.exp(jax.random.uniform(key_cols, (D,), jnp.float32, -0.7, 0.7))
    column_scale = 0.6 * jnp.power(3.0, position) * roughness
    row_scale = jnp.exp(jax.random.uniform(key_rows, (TOKENS, 1), jnp.float32, math.log(0.3), math.log(3.0)))
    base = jnp.clip(jax.random.normal(key_base, (TOKENS, D), jnp.float32), -4.0, 4.0)
    return (base * column_scale * row_scale).astype(jnp.bfloat16)


def block_levels(rng, extent, shards, least, largest):
    gain, own = 1.0, jax.random.fold_in(rng, 6)
    for axis_at, blocks in shards:
        heights = jnp.exp(jax.random.uniform(jax.random.fold_in(own, axis_at), (blocks,), jnp.float32, least / len(shards), largest / len(shards)))
        gain = gain * jnp.repeat(heights, extent[axis_at] // blocks).reshape([-1 if axis == axis_at else 1 for axis in range(len(extent))])
    return gain


def shared_out(rng, own, number, rows, count, top, reach, lean):
    order = jax.random.permutation(rng, count)
    heavy_load, common = load_shares(count, rows * top, reach, lean, True), load_shares(count, rows * top, reach, lean, False)
    places = jnp.arange(count)

    def named(lengths, offset_by):
        used = int((lengths > 0).sum())
        fixed = max(1, used // 4)
        moved = fixed + (places - fixed + offset_by * (used - fixed)) % max(1, count - fixed)
        return jnp.zeros((count,), jnp.int32).at[order[jnp.where(places < fixed, places, moved)]].set(jnp.asarray(lengths, jnp.int32))

    lengths = jnp.where(number % 4 == 0, named(heavy_load, number // 4), named(common, number - number // 4 - 1))
    mixed = jax.random.permutation(jax.random.fold_in(own, 3), count)
    source_of, sink = mixed[0:count // 2 * 2:2], mixed[1:count // 2 * 2:2]
    margin = jnp.minimum(lengths[source_of] - 1, reach - lengths[sink]) // 2
    margin = jnp.where((source_of == order[0]) | (sink == order[0]) | (lengths[sink] == 0), 0, jnp.maximum(margin, 0))
    moved = jax.random.randint(jax.random.fold_in(own, 4), (count // 2,), 0, 1 << 20) % (margin + 1)
    lengths = lengths.at[source_of].add(-moved).at[sink].add(moved)
    members = jnp.searchsorted(jnp.cumsum(lengths), jnp.arange(rows * top), side="right").astype(jnp.int32)
    grid = members.reshape(top, rows).T
    grid = grid[jax.random.permutation(jax.random.fold_in(own, 1), rows)]
    offset_by = jax.random.randint(jax.random.fold_in(own, 2), (rows, 1), 0, top)
    return jnp.take_along_axis(grid, (jnp.arange(top)[None, :] + offset_by) % top, axis=1)


def load_shares(count, total, reach, slope, full):
    portions = [(1 << 20) // math.isqrt(standing ** slope) + 1 for standing in range(1, count + 1)]
    largest = reach if full else min(reach, max(-(-total // count), total * portions[0] // sum(portions)))
    least = 1 if total - largest >= count - 1 else 0
    counts, rest = [largest] + [least] * (count - 1), total - largest - least * (count - 1)
    while rest > 0:
        movable = [i for i in range(1, count) if counts[i] < largest] or [i for i in range(1, count) if counts[i] < reach]
        whole, budget = sum([portions[i] for i in movable]), rest
        for i in movable:
            extra = min(reach - counts[i], max(1, budget * portions[i] // whole), rest)
            counts[i] = counts[i] + extra
            rest = rest - extra
    return np.array(counts)


def bell_draw(stream_key, dims, width, limit, cuts=(), kind=jnp.bfloat16):
    array = jax.random.normal(stream_key, dims, jnp.float32) * width
    if len(cuts) > 0:
        array = block_levels(stream_key, dims, cuts, -0.22, 0.18) * array
    return jnp.clip(array, min=-limit, max=limit).astype(kind)


def setup_inputs(seed: int = 0) -> dict:
    streams_of = jax.random.split(jax.random.key(seed), 9)
    tokens = draw_tokens(jax.random.fold_in(streams_of[8], 71), 0)
    norm_gain = jnp.clip(1.0 + 0.18 * jax.random.normal(streams_of[1], (D,), jnp.float32), 0.1, 1.9)
    w_gate = bell_draw(streams_of[2], (EXPERTS, D, HID), D ** -0.5, 0.0625, ((0, 8), (2, 4)))
    w_up = bell_draw(streams_of[3], (EXPERTS, D, HID), D ** -0.5, 0.0625, ((0, 8), (2, 4)))
    w_down = bell_draw(streams_of[4], (EXPERTS, HID, D), HID ** -0.5, 0.125, ((0, 8), (1, 4)))
    regions_keys = jax.random.split(jax.random.fold_in(streams_of[5], 1), TOKENS // T_DEV)
    regions_turns = jax.random.permutation(jax.random.fold_in(streams_of[5], 3), TOKENS // T_DEV)
    regions = jax.vmap(lambda own, number: shared_out(jax.random.fold_in(streams_of[5], 2), own, number, T_DEV, N_REGION, TOP, CAP, 2))(regions_keys, regions_turns).reshape((TOKENS, TOP))
    combine = jnp.clip(jnp.exp(math.log(1.0) - 2.3025851 * jax.random.uniform(streams_of[6], (TOKENS, TOP), jnp.float32) ** block_levels(streams_of[6], (TOKENS, TOP), ((0, 8),), -0.2, 0.2)), 0.1, 1.0)
    grad_out = bell_draw(streams_of[7], (TOKENS, D), 0.5, 3.0, ((0, 8), (1, 4)))
    return dict(tokens=tokens, norm_gain=norm_gain, w_gate=w_gate, w_up=w_up, w_down=w_down, regions=regions, combine=combine, grad_out=grad_out)


def reference(tokens, norm_gain, w_gate, w_up, w_down, regions, combine, grad_out):
    inputs_f32 = tokens.astype(jnp.float32)
    sum_squares = lax.optimization_barrier(jnp.sum(inputs_f32 * inputs_f32, axis=1, keepdims=True))
    inv_rms = lax.rsqrt(sum_squares / D + 1e-06)
    gain_f32 = norm_gain.astype(jnp.float32)
    normed = (inputs_f32 * inv_rms * gain_f32).astype(jnp.bfloat16)
    flat_routes = regions.reshape(-1)
    flat_weights = combine.reshape(-1)
    most_rows = N_REGION * CAP

    def one_expert(expert, carry):
        out_total, grad_total, comb_total = carry
        chosen = flat_routes == expert
        index = jnp.nonzero(chosen, size=most_rows, fill_value=0)[0].astype(jnp.int32)
        live = (jnp.arange(most_rows) < jnp.sum(chosen.astype(jnp.int32))).astype(jnp.float32)
        owner = index // TOP
        rows_in = normed[owner]
        rows_grad = grad_out[owner]
        gate_w = w_gate[expert]
        up_w = w_up[expert]
        down_w = w_down[expert]
        gate_pre = jnp.dot(rows_in, gate_w, preferred_element_type=jnp.float32)
        up_pre = jnp.dot(rows_in, up_w, preferred_element_type=jnp.float32)
        sig_gate = jax.nn.sigmoid(gate_pre)
        act_gate = gate_pre * sig_gate
        hidden = (act_gate * up_pre).astype(jnp.bfloat16)
        expert_out = jnp.dot(hidden, down_w, preferred_element_type=jnp.float32)
        grad_hidden = jnp.dot(rows_grad, down_w.T, preferred_element_type=jnp.float32)
        grad_gate = (grad_hidden * up_pre * sig_gate * (1.0 + gate_pre * (1.0 - sig_gate))).astype(jnp.bfloat16)
        grad_up = (grad_hidden * act_gate).astype(jnp.bfloat16)
        branch_grad = jnp.dot(grad_gate, gate_w.T, preferred_element_type=jnp.float32) + jnp.dot(grad_up, up_w.T, preferred_element_type=jnp.float32)
        weight_live = flat_weights[index] * live
        out_total = out_total.at[owner].add(weight_live[:, None] * expert_out)
        grad_total = grad_total.at[owner].add(weight_live[:, None] * branch_grad)
        comb_piece = lax.optimization_barrier(jnp.sum(rows_grad.astype(jnp.float32) * expert_out, axis=1)) * live
        comb_total = comb_total.at[index].add(comb_piece)
        return (out_total, grad_total, comb_total)
    start = (jnp.zeros((TOKENS, D), jnp.float32), jnp.zeros((TOKENS, D), jnp.float32), jnp.zeros((TOKENS * TOP,), jnp.float32))
    out_total, grad_total, comb_total = lax.fori_loop(0, N_REGION, one_expert, start)
    moe_out = out_total.astype(jnp.bfloat16)
    scaled = gain_f32 * grad_total
    inner = lax.optimization_barrier(jnp.sum(inputs_f32 * scaled, axis=1, keepdims=True))
    grad_tokens = (inv_rms * scaled - inputs_f32 * inv_rms * inv_rms * inv_rms * inner / D).astype(jnp.bfloat16)
    grad_combine = comb_total.reshape(TOKENS, TOP)
    return (moe_out, grad_tokens, grad_combine)
```

```python
import jax
import jax.numpy as jnp
from jax import lax
from jax.sharding import PartitionSpec as P

D = 7168
F32 = jnp.float32
BF16 = jnp.bfloat16
LAST = (((1,), (1,)), ((), ()))


def dot(left, right):
    return jnp.dot(left, right, preferred_element_type=F32)


def split_weights(weights):
    high = weights.astype(BF16)
    return high, (weights - high.astype(F32)).astype(BF16)


def on_device(tokens, norm_gain, w_gate, w_up, w_down, regions, combine, grad_out):
    token_count, width_local = tokens.shape
    region_count = lax.axis_size("region")
    route_count = regions.shape[1]
    capacity = max(2, token_count * route_count * 5 // (4 * region_count))
    slot_total = region_count * capacity
    gate_w, up_w, down_w = w_gate[0], w_up[0], w_down[0]

    gain_full = lax.all_gather(norm_gain, "local", axis=0, tiled=True)
    tokens_full = lax.all_gather(tokens, "local", axis=1, tiled=True)
    grad_full = lax.all_gather(grad_out, "local", axis=1, tiled=True)

    flat_routes = regions.reshape(-1)
    one_hot = (flat_routes[:, None] == jnp.arange(region_count, dtype=jnp.int32)[None, :]).astype(F32)
    pairs = token_count * route_count
    earlier = (jnp.arange(pairs)[:, None] > jnp.arange(pairs)[None, :]).astype(F32)
    running = dot(earlier.astype(BF16), one_hot.astype(BF16))
    slot_index = jnp.sum(running * one_hot, axis=1).astype(jnp.int32)
    placement = (flat_routes * capacity + slot_index).reshape(token_count, route_count)
    hits = placement[:, :, None] == jnp.arange(slot_total, dtype=jnp.int32)[None, None, :]
    spread = jnp.sum(hits.astype(F32), axis=1).astype(BF16)
    weighted = jnp.sum(jnp.where(hits, combine[:, :, None], 0.0), axis=1)
    weight_high, weight_low = split_weights(weighted)

    def pack_rows(matrix):
        picked = lax.dot_general(spread, matrix, (((0,), (0,)), ((), ())), preferred_element_type=F32)
        return picked.astype(BF16).reshape(region_count, capacity, matrix.shape[1])

    def exchange(blocks):
        return lax.all_to_all(blocks, "region", split_axis=0, concat_axis=0, tiled=True)

    inputs_full = tokens_full.astype(F32)
    inv_rms = lax.rsqrt(jnp.sum(inputs_full * inputs_full, axis=1, keepdims=True) / D + 1e-06)
    normed = (inputs_full * inv_rms * gain_full).astype(BF16)
    rows_in = exchange(pack_rows(normed)).reshape(slot_total, D)
    rows_grad = exchange(pack_rows(grad_full)).reshape(slot_total, D)

    gate_pre = dot(rows_in, gate_w)
    up_pre = dot(rows_in, up_w)
    sig_gate = jax.nn.sigmoid(gate_pre)
    act_gate = gate_pre * sig_gate
    hidden = (act_gate * up_pre).astype(BF16)
    expert_out = dot(hidden, down_w).astype(BF16)
    grad_hidden = lax.dot_general(rows_grad, down_w, LAST, preferred_element_type=F32)
    grad_gate = (grad_hidden * up_pre * sig_gate * (1.0 + gate_pre * (1.0 - sig_gate))).astype(BF16)
    grad_up = (grad_hidden * act_gate).astype(BF16)
    branch_grad = (
        lax.dot_general(grad_gate, gate_w, LAST, preferred_element_type=F32)
        + lax.dot_general(grad_up, up_w, LAST, preferred_element_type=F32)
    ).astype(BF16)

    comb_part = jnp.sum(hidden.astype(F32) * grad_hidden, axis=1)
    inner_part = jnp.sum(grad_gate.astype(F32) * gate_pre + grad_up.astype(F32) * up_pre, axis=1)

    back_out = exchange(expert_out.reshape(region_count, capacity, D)).reshape(slot_total, D)
    out_sum = dot(weight_high, back_out) + dot(weight_low, back_out)
    moe_out = lax.psum_scatter(out_sum.astype(BF16), "local", scatter_dimension=1, tiled=True)

    scalars = exchange(jnp.stack([comb_part, inner_part], axis=1).reshape(region_count, capacity, 2))
    scalars = scalars.reshape(slot_total, 2)
    picked = jnp.sum(jnp.where(hits[:, :, :, None], scalars[None, None, :, :], 0.0), axis=2)
    picked = lax.psum(picked, "local")
    grad_combine = picked[:, :, 0]
    inner = jnp.sum(picked[:, :, 1] * combine, axis=1, keepdims=True) / inv_rms

    back_grad = exchange(branch_grad.reshape(region_count, capacity, D)).reshape(slot_total, D)
    grad_sum = dot(weight_high, back_grad) + dot(weight_low, back_grad)
    grad_normed = lax.psum_scatter(grad_sum.astype(BF16), "local", scatter_dimension=1, tiled=True)
    scaled = norm_gain * grad_normed.astype(F32)
    grad_tokens = (
        inv_rms * scaled - tokens.astype(F32) * inv_rms * inv_rms * inv_rms * inner / D
    ).astype(BF16)
    return (moe_out, grad_tokens, grad_combine)


def solution(mesh):
    placed = (
        P("region", "local"),
        P("local"),
        P("region", None, "local"),
        P("region", None, "local"),
        P("region", "local", None),
        P("region", None),
        P("region", None),
        P("region", "local"),
    )
    return jax.shard_map(
        on_device,
        mesh=mesh,
        in_specs=placed,
        out_specs=(P("region", "local"), P("region", "local"), P("region", None)),
        check_vma=False,
    )
```

```python
import jax
import jax.numpy as jnp
from jax import lax
from jax.sharding import PartitionSpec as P

D = 7168
F32 = jnp.float32
BF16 = jnp.bfloat16
LAST = (((1,), (1,)), ((), ()))


def dot(left, right):
    return jnp.dot(left, right, preferred_element_type=F32)


def split_weights(weights):
    high = weights.astype(BF16)
    return high, (weights - high.astype(F32)).astype(BF16)


def on_device(tokens, norm_gain, w_gate, w_up, w_down, regions, combine, grad_out):
    token_count, width_local = tokens.shape
    region_count = lax.axis_size("region")
    route_count = regions.shape[1]
    capacity = max(2, token_count * route_count * 5 // (4 * region_count))
    slot_total = region_count * capacity
    gate_w, up_w, down_w = w_gate[0], w_up[0], w_down[0]

    near = width_local // 256 * 128
    far = width_local - near
    share_count = lax.axis_size("local")

    def gather(matrix):
        return lax.all_gather(matrix, "local", axis=1, tiled=True)

    def scatter(matrix):
        width = matrix.shape[1] // share_count
        stacked = jnp.stack([matrix[:, z * width:(z + 1) * width] for z in range(share_count)])
        return lax.psum_scatter(stacked, "local", scatter_dimension=0, tiled=False)

    def columns(matrix, start, width):
        cuts = [lax.slice_in_dim(matrix, z * width_local + start, z * width_local + start + width, axis=1) for z in range(share_count)]
        return jnp.concatenate(cuts, axis=1)

    flat_routes = regions.reshape(-1)
    one_hot = (flat_routes[:, None] == jnp.arange(region_count, dtype=jnp.int32)[None, :]).astype(F32)
    pairs = token_count * route_count
    earlier = (jnp.arange(pairs)[:, None] > jnp.arange(pairs)[None, :]).astype(F32)
    running = dot(earlier.astype(BF16), one_hot.astype(BF16))
    slot_index = jnp.sum(running * one_hot, axis=1).astype(jnp.int32)
    placement = (flat_routes * capacity + slot_index).reshape(token_count, route_count)
    hits = placement[:, :, None] == jnp.arange(slot_total, dtype=jnp.int32)[None, None, :]
    spread = jnp.sum(hits.astype(F32), axis=1).astype(BF16)
    weighted = jnp.sum(jnp.where(hits, combine[:, :, None], 0.0), axis=1)
    weight_high, weight_low = split_weights(weighted)

    def pack_rows(matrix):
        picked = lax.dot_general(spread, matrix, (((0,), (0,)), ((), ())), preferred_element_type=F32)
        return picked.astype(BF16).reshape(region_count, capacity, matrix.shape[1])

    def exchange(blocks):
        return lax.all_to_all(blocks, "region", split_axis=0, concat_axis=0, tiled=True)

    grad_near = gather(grad_out[:, :near])
    far_blocks = exchange(pack_rows(grad_out[:, near:])).reshape(slot_total, far)
    gain_high, gain_rest = split_weights(norm_gain)
    gain_mid, gain_low = split_weights(norm_gain - gain_high.astype(F32))
    gain_rows = jnp.stack([gain_high, gain_mid, gain_low])
    tokens_cat = jnp.concatenate([tokens, jnp.pad(gain_rows, ((0, 5), (0, 0)))], axis=0)
    tokens_cat, grad_near = lax.optimization_barrier((tokens_cat, grad_near))
    tokens_full = gather(tokens_cat)
    near_rows = exchange(pack_rows(grad_near)).reshape(slot_total, share_count * near)
    far_blocks, tokens_full = lax.optimization_barrier((far_blocks, tokens_full))
    far_rows = gather(far_blocks)

    gain_full = jnp.sum(tokens_full[token_count:token_count + 3].astype(F32), axis=0)
    inputs_full = tokens_full[:token_count].astype(F32)
    inv_rms = lax.rsqrt(jnp.sum(inputs_full * inputs_full, axis=1, keepdims=True) / D + 1e-06)
    normed = (inputs_full * inv_rms * gain_full).astype(BF16)
    rows_in = exchange(pack_rows(normed)).reshape(slot_total, D)
    pieces = []
    for z in range(share_count):
        pieces.append(near_rows[:, z * near:(z + 1) * near])
        pieces.append(far_rows[:, z * far:(z + 1) * far])
    rows_grad = jnp.concatenate(pieces, axis=1)

    gate_pre = dot(rows_in, gate_w)
    up_pre = dot(rows_in, up_w)
    sig_gate = jax.nn.sigmoid(gate_pre)
    act_gate = gate_pre * sig_gate
    hidden = (act_gate * up_pre).astype(BF16)
    expert_out = dot(hidden, down_w).astype(BF16)
    grad_hidden = lax.dot_general(rows_grad, down_w, LAST, preferred_element_type=F32)
    grad_gate = (grad_hidden * up_pre * sig_gate * (1.0 + gate_pre * (1.0 - sig_gate))).astype(BF16)
    grad_up = (grad_hidden * act_gate).astype(BF16)
    branch_grad = (
        lax.dot_general(grad_gate, gate_w, LAST, preferred_element_type=F32)
        + lax.dot_general(grad_up, up_w, LAST, preferred_element_type=F32)
    ).astype(BF16)

    comb_part = jnp.sum(hidden.astype(F32) * grad_hidden, axis=1)
    inner_part = jnp.sum(grad_gate.astype(F32) * gate_pre + grad_up.astype(F32) * up_pre, axis=1)

    scalars = jnp.stack([comb_part, inner_part], axis=1)
    scalars = jnp.concatenate(split_weights(scalars), axis=1)
    scalars = jnp.pad(scalars, ((0, 0), (0, 124)))

    def send_home(rows):
        return exchange(rows.reshape(region_count, capacity, rows.shape[1])).reshape(slot_total, rows.shape[1])

    def combined(rows):
        return dot(weight_high, rows) + dot(weight_low, rows)

    out_far = scatter(columns(expert_out, near, far))
    near_sent = jnp.concatenate([columns(expert_out, 0, near), scalars], axis=1)
    out_near = send_home(near_sent)
    early = send_home(columns(branch_grad, 0, near))
    out_near, out_far = lax.optimization_barrier((out_near, out_far))
    scalars = out_near[:, share_count * near:]
    picked = jnp.einsum("tks,sc->tkc", hits.astype(BF16), scalars, preferred_element_type=F32)
    picked = lax.psum(picked[:, :, :2] + picked[:, :, 2:4], "local")
    grad_combine = picked[:, :, 0]
    inner = jnp.sum(picked[:, :, 1] * combine, axis=1, keepdims=True) / inv_rms

    moe_near = scatter(combined(out_near[:, :share_count * near]).astype(BF16))
    out_far, early = lax.optimization_barrier((out_far, early))
    back_far = send_home(out_far)
    moe_far = combined(back_far).astype(BF16)
    moe_out = jnp.concatenate([moe_near, moe_far], axis=1)

    early = combined(early).astype(BF16)
    late, back_far, early = lax.optimization_barrier((columns(branch_grad, near, far), back_far, early))
    early = scatter(early)
    late = send_home(late)
    late, inner = lax.optimization_barrier((late, inner))
    late = scatter(combined(late).astype(BF16))
    grad_normed = jnp.concatenate([early, late], axis=1)
    scaled = norm_gain * grad_normed.astype(F32)
    grad_tokens = (
        inv_rms * scaled - tokens.astype(F32) * inv_rms * inv_rms * inv_rms * inner / D
    ).astype(BF16)
    return (moe_out, grad_tokens, grad_combine)


def solution(mesh):
    placed = (
        P("region", "local"),
        P("local"),
        P("region", None, "local"),
        P("region", None, "local"),
        P("region", "local", None),
        P("region", None),
        P("region", None),
        P("region", "local"),
    )
    return jax.shard_map(
        on_device,
        mesh=mesh,
        in_specs=placed,
        out_specs=(P("region", "local"), P("region", "local"), P("region", None)),
        check_vma=False,
    )
```

```python
import jax
import jax.numpy as jnp
from jax import lax
from jax.sharding import PartitionSpec as P

D = 7168
F32 = jnp.float32
BF16 = jnp.bfloat16
LAST = (((1,), (1,)), ((), ()))


def dot(left, right):
    return jnp.dot(left, right, preferred_element_type=F32)


def split_weights(weights):
    high = weights.astype(BF16)
    return high, (weights - high.astype(F32)).astype(BF16)


def on_device(tokens, norm_gain, w_gate, w_up, w_down, regions, combine, grad_out):
    token_count, width_local = tokens.shape
    region_count = lax.axis_size("region")
    route_count = regions.shape[1]
    capacity = max(2, token_count * route_count * 5 // (4 * region_count))
    slot_total = region_count * capacity
    gate_w, up_w, down_w = w_gate[0], w_up[0], w_down[0]

    share_count = lax.axis_size("local")

    def gather(matrix):
        return lax.all_gather(matrix, "local", axis=1, tiled=True)

    def scatter(matrix):
        width = matrix.shape[1] // share_count
        stacked = jnp.stack([matrix[:, z * width:(z + 1) * width] for z in range(share_count)])
        return lax.psum_scatter(stacked, "local", scatter_dimension=0, tiled=False)

    flat_routes = regions.reshape(-1)
    one_hot = (flat_routes[:, None] == jnp.arange(region_count, dtype=jnp.int32)[None, :]).astype(F32)
    pairs = token_count * route_count
    earlier = (jnp.arange(pairs)[:, None] > jnp.arange(pairs)[None, :]).astype(F32)
    running = dot(earlier.astype(BF16), one_hot.astype(BF16))
    slot_index = jnp.sum(running * one_hot, axis=1).astype(jnp.int32)
    placement = (flat_routes * capacity + slot_index).reshape(token_count, route_count)
    hits = placement[:, :, None] == jnp.arange(slot_total, dtype=jnp.int32)[None, None, :]
    spread = jnp.sum(hits.astype(F32), axis=1).astype(BF16)
    weighted = jnp.sum(jnp.where(hits, combine[:, :, None], 0.0), axis=1)
    weight_high, weight_low = split_weights(weighted)

    def pack_rows(matrix):
        picked = lax.dot_general(spread, matrix, (((0,), (0,)), ((), ())), preferred_element_type=F32)
        return picked.astype(BF16).reshape(region_count, capacity, matrix.shape[1])

    def exchange(blocks):
        return lax.all_to_all(blocks, "region", split_axis=0, concat_axis=0, tiled=True)

    far_blocks = exchange(pack_rows(grad_out)).reshape(slot_total, width_local)
    gain_high, gain_rest = split_weights(norm_gain)
    gain_mid, gain_low = split_weights(norm_gain - gain_high.astype(F32))
    gain_rows = jnp.stack([gain_high, gain_mid, gain_low])
    tokens_cat = jnp.concatenate([tokens, jnp.pad(gain_rows, ((0, 5), (0, 0)))], axis=0)
    tokens_full = gather(tokens_cat)
    far_blocks, tokens_full = lax.optimization_barrier((far_blocks, tokens_full))
    rows_grad = gather(far_blocks)

    gain_full = jnp.sum(tokens_full[token_count:token_count + 3].astype(F32), axis=0)
    inputs_full = tokens_full[:token_count].astype(F32)
    inv_rms = lax.rsqrt(jnp.sum(inputs_full * inputs_full, axis=1, keepdims=True) / D + 1e-06)
    normed = (inputs_full * inv_rms * gain_full).astype(BF16)
    rows_in = exchange(pack_rows(normed)).reshape(slot_total, D)
    gate_pre = dot(rows_in, gate_w)
    up_pre = dot(rows_in, up_w)
    sig_gate = jax.nn.sigmoid(gate_pre)
    act_gate = gate_pre * sig_gate
    hidden = (act_gate * up_pre).astype(BF16)
    expert_out = dot(hidden, down_w).astype(BF16)
    grad_hidden = lax.dot_general(rows_grad, down_w, LAST, preferred_element_type=F32)
    grad_gate = (grad_hidden * up_pre * sig_gate * (1.0 + gate_pre * (1.0 - sig_gate))).astype(BF16)
    grad_up = (grad_hidden * act_gate).astype(BF16)
    expert_out, grad_gate, grad_up = lax.optimization_barrier((expert_out, grad_gate, grad_up))
    branch_grad = (
        lax.dot_general(grad_gate, gate_w, LAST, preferred_element_type=F32)
        + lax.dot_general(grad_up, up_w, LAST, preferred_element_type=F32)
    ).astype(BF16)

    comb_part = jnp.sum(hidden.astype(F32) * grad_hidden, axis=1)
    inner_part = jnp.sum(grad_gate.astype(F32) * gate_pre + grad_up.astype(F32) * up_pre, axis=1)

    scalars = jnp.stack([comb_part, inner_part], axis=1)
    scalars = jnp.concatenate(split_weights(scalars), axis=1)
    scalars = jnp.pad(scalars, ((0, 0), (0, 124)))

    def send_home(rows):
        return exchange(rows.reshape(region_count, capacity, rows.shape[1])).reshape(slot_total, rows.shape[1])

    def combined(rows):
        return dot(weight_high, rows) + dot(weight_low, rows)

    out_share = scatter(expert_out)
    back_grad = send_home(jnp.concatenate([branch_grad, scalars], axis=1))
    picked = jnp.einsum("tks,sc->tkc", hits.astype(BF16), back_grad[:, D:], preferred_element_type=F32)
    picked = lax.psum(picked[:, :, :2] + picked[:, :, 2:4], "local")
    grad_combine = picked[:, :, 0]
    inner = jnp.sum(picked[:, :, 1] * combine, axis=1, keepdims=True) / inv_rms
    grad_sum = combined(back_grad[:, :D]).astype(BF16)
    grad_sum, out_share = lax.optimization_barrier((grad_sum, out_share))
    grad_normed = scatter(grad_sum)
    moe_out = combined(send_home(out_share)).astype(BF16)
    scaled = norm_gain * grad_normed.astype(F32)
    grad_tokens = (
        inv_rms * scaled - tokens.astype(F32) * inv_rms * inv_rms * inv_rms * inner / D
    ).astype(BF16)
    return (moe_out, grad_tokens, grad_combine)


def solution(mesh):
    placed = (
        P("region", "local"),
        P("local"),
        P("region", None, "local"),
        P("region", None, "local"),
        P("region", "local", None),
        P("region", None),
        P("region", None),
        P("region", "local"),
    )
    return jax.shard_map(
        on_device,
        mesh=mesh,
        in_specs=placed,
        out_specs=(P("region", "local"), P("region", "local"), P("region", None)),
        check_vma=False,
    )
```

```python
import functools

import jax
import jax.numpy as jnp
from jax import lax
from jax.experimental import pallas as pl
from jax.experimental.pallas import tpu as pltpu
from jax.sharding import PartitionSpec as P

D = 7168
F32 = jnp.float32
BF16 = jnp.bfloat16
LAST = (((1,), (1,)), ((), ()))


def dot(left, right):
    return jnp.dot(left, right, preferred_element_type=F32)


def split_weights(weights):
    high = weights.astype(BF16)
    return high, (weights - high.astype(F32)).astype(BF16)


def spread_kernel(share, regions, near_ref, far_ref, near_out, far_out, up_send, up_recv, down_send, down_recv, far_send, far_recv, own_sem):
    region, z = lax.axis_index("region"), lax.axis_index("local")
    width = near_ref.shape[1]
    has_above, has_below = z + 1 < share, z >= 1

    barrier = pltpu.get_barrier_semaphore()

    def greet(there):
        pl.semaphore_signal(barrier, inc=1, device_id=there, device_id_type=pl.DeviceIdType.MESH)

    for offset in range(1, regions):
        greet((lax.rem(region + offset, regions), z))
    pl.when(has_above)(lambda: greet((region, z + 1)))
    pl.when(has_below)(lambda: greet((region, z - 1)))
    inside = has_above & has_below
    pl.when(inside)(lambda: pl.semaphore_wait(barrier, regions + 1))
    pl.when(jnp.logical_not(inside))(lambda: pl.semaphore_wait(barrier, regions))

    def slot(owner):
        return near_out.at[:, pl.ds(pl.multiple_of(owner * width, 128), width)]

    def hop(step, way):
        owner = z - step * way
        send, recv = (up_send, up_recv) if way > 0 else (down_send, down_recv)
        return pltpu.make_async_remote_copy(
            src_ref=near_ref if step == 0 else slot(owner),
            dst_ref=slot(owner),
            send_sem=send.at[step],
            recv_sem=recv.at[step],
            device_id=(region, z + way),
            device_id_type=pl.DeviceIdType.MESH,
        )

    def landed(step, way):
        owner = z - (step + 1) * way
        send, recv = (up_send, up_recv) if way > 0 else (down_send, down_recv)
        pltpu.make_async_remote_copy(
            src_ref=slot(owner),
            dst_ref=slot(owner),
            send_sem=send.at[step],
            recv_sem=recv.at[step],
            device_id=(region, z + way),
            device_id_type=pl.DeviceIdType.MESH,
        ).wait_recv()

    def sends(step, way):
        owner = z - step * way
        there = has_above if way > 0 else has_below
        return there & (owner >= 0) & (owner < share)

    def parcel(offset):
        peer = lax.rem(region + offset, regions)
        return pltpu.make_async_remote_copy(
            src_ref=far_ref.at[peer],
            dst_ref=far_out.at[region],
            send_sem=far_send.at[offset],
            recv_sem=far_recv.at[offset],
            device_id=(peer, z),
            device_id_type=pl.DeviceIdType.MESH,
        )

    for way in (1, -1):
        pl.when(sends(0, way))(lambda way=way: hop(0, way).start())
    for offset in range(1, regions):
        parcel(offset).start()
    own_near = pltpu.make_async_copy(near_ref, slot(z), own_sem.at[0])
    own_far = pltpu.make_async_copy(far_ref.at[region], far_out.at[region], own_sem.at[1])
    own_near.start()
    own_far.start()
    for step in range(1, share):
        for way in (1, -1):
            owner = z - step * way
            pl.when((owner >= 0) & (owner < share))(lambda step=step, way=way: landed(step - 1, way))
            if step < share - 1:
                pl.when(sends(step, way))(lambda step=step, way=way: hop(step, way).start())
    for step in range(share - 1):
        for way in (1, -1):
            pl.when(sends(step, way))(lambda step=step, way=way: hop(step, way).wait_send())
    for offset in range(1, regions):
        parcel(offset).wait()
    own_near.wait()
    own_far.wait()


def spread_out(number, near, far):
    share, regions = lax.axis_size("local"), lax.axis_size("region")
    rows, width = near.shape
    moved = 2 * (rows * width * share + 2 * far.size)
    return pl.pallas_call(
        functools.partial(spread_kernel, share, regions),
        out_shape=(
            jax.ShapeDtypeStruct((rows, width * share), near.dtype),
            jax.ShapeDtypeStruct(far.shape, far.dtype),
        ),
        in_specs=[pl.BlockSpec(memory_space=pl.ANY)] * 2,
        out_specs=[pl.BlockSpec(memory_space=pl.ANY)] * 2,
        scratch_shapes=[pltpu.SemaphoreType.DMA((share,))] * 4
        + [pltpu.SemaphoreType.DMA((regions,))] * 2
        + [pltpu.SemaphoreType.DMA((2,))],
        compiler_params=pltpu.CompilerParams(collective_id=number, has_side_effects=True),
        cost_estimate=pl.CostEstimate(flops=0, bytes_accessed=moved, transcendentals=0),
    )(near, far)


def on_device(tokens, norm_gain, w_gate, w_up, w_down, regions, combine, grad_out):
    token_count, width_local = tokens.shape
    region_count = lax.axis_size("region")
    route_count = regions.shape[1]
    capacity = max(2, token_count * route_count * 5 // (4 * region_count))
    slot_total = region_count * capacity
    gate_w, up_w, down_w = w_gate[0], w_up[0], w_down[0]

    share_count = lax.axis_size("local")

    def scatter(matrix):
        width = matrix.shape[1] // share_count
        stacked = jnp.stack([matrix[:, z * width:(z + 1) * width] for z in range(share_count)])
        return lax.psum_scatter(stacked, "local", scatter_dimension=0, tiled=False)

    flat_routes = regions.reshape(-1)
    one_hot = (flat_routes[:, None] == jnp.arange(region_count, dtype=jnp.int32)[None, :]).astype(F32)
    pairs = token_count * route_count
    earlier = (jnp.arange(pairs)[:, None] > jnp.arange(pairs)[None, :]).astype(F32)
    running = dot(earlier.astype(BF16), one_hot.astype(BF16))
    slot_index = jnp.sum(running * one_hot, axis=1).astype(jnp.int32)
    placement = (flat_routes * capacity + slot_index).reshape(token_count, route_count)
    hits = placement[:, :, None] == jnp.arange(slot_total, dtype=jnp.int32)[None, None, :]
    spread = jnp.sum(hits.astype(F32), axis=1).astype(BF16)
    weighted = jnp.sum(jnp.where(hits, combine[:, :, None], 0.0), axis=1)
    weight_high, weight_low = split_weights(weighted)

    def pack_rows(matrix):
        picked = lax.dot_general(spread, matrix, (((0,), (0,)), ((), ())), preferred_element_type=F32)
        return picked.astype(BF16).reshape(region_count, capacity, matrix.shape[1])

    def exchange(blocks):
        return lax.all_to_all(blocks, "region", split_axis=0, concat_axis=0, tiled=True)

    gain_high, gain_rest = split_weights(norm_gain)
    gain_mid, gain_low = split_weights(norm_gain - gain_high.astype(F32))
    gain_rows = jnp.stack([gain_high, gain_mid, gain_low])
    tokens_cat = jnp.concatenate([tokens, jnp.pad(gain_rows, ((0, 13), (0, 0)))], axis=0)
    tokens_full, far_blocks = spread_out(0, tokens_cat, pack_rows(grad_out))

    gain_full = jnp.sum(tokens_full[token_count:token_count + 3].astype(F32), axis=0)
    inputs_full = tokens_full[:token_count].astype(F32)
    inv_rms = lax.rsqrt(jnp.sum(inputs_full * inputs_full, axis=1, keepdims=True) / D + 1e-06)
    normed = (inputs_full * inv_rms * gain_full).astype(BF16)
    rows_grad, rows_in = spread_out(1, far_blocks.reshape(slot_total, width_local), pack_rows(normed))
    rows_in = rows_in.reshape(slot_total, D)
    gate_pre = dot(rows_in, gate_w)
    up_pre = dot(rows_in, up_w)
    sig_gate = jax.nn.sigmoid(gate_pre)
    act_gate = gate_pre * sig_gate
    hidden = (act_gate * up_pre).astype(BF16)
    expert_out = dot(hidden, down_w).astype(BF16)
    grad_hidden = lax.dot_general(rows_grad, down_w, LAST, preferred_element_type=F32)
    grad_gate = (grad_hidden * up_pre * sig_gate * (1.0 + gate_pre * (1.0 - sig_gate))).astype(BF16)
    grad_up = (grad_hidden * act_gate).astype(BF16)
    expert_out, grad_gate, grad_up = lax.optimization_barrier((expert_out, grad_gate, grad_up))
    branch_grad = (
        lax.dot_general(grad_gate, gate_w, LAST, preferred_element_type=F32)
        + lax.dot_general(grad_up, up_w, LAST, preferred_element_type=F32)
    ).astype(BF16)

    comb_part = jnp.sum(hidden.astype(F32) * grad_hidden, axis=1)
    inner_part = jnp.sum(grad_gate.astype(F32) * gate_pre + grad_up.astype(F32) * up_pre, axis=1)

    scalars = jnp.stack([comb_part, inner_part], axis=1)
    scalars = jnp.concatenate(split_weights(scalars), axis=1)
    scalars = jnp.pad(scalars, ((0, 0), (0, 124)))

    def send_home(rows):
        return exchange(rows.reshape(region_count, capacity, rows.shape[1])).reshape(slot_total, rows.shape[1])

    def combined(rows):
        return dot(weight_high, rows) + dot(weight_low, rows)

    out_share = scatter(expert_out)
    back_grad = send_home(jnp.concatenate([branch_grad, scalars], axis=1))
    picked = jnp.einsum("tks,sc->tkc", hits.astype(BF16), back_grad[:, D:], preferred_element_type=F32)
    picked = lax.psum(picked[:, :, :2] + picked[:, :, 2:4], "local")
    grad_combine = picked[:, :, 0]
    inner = jnp.sum(picked[:, :, 1] * combine, axis=1, keepdims=True) / inv_rms
    grad_sum = combined(back_grad[:, :D]).astype(BF16)
    grad_sum, out_share = lax.optimization_barrier((grad_sum, out_share))
    grad_normed = scatter(grad_sum)
    moe_out = combined(send_home(out_share)).astype(BF16)
    scaled = norm_gain * grad_normed.astype(F32)
    grad_tokens = (
        inv_rms * scaled - tokens.astype(F32) * inv_rms * inv_rms * inv_rms * inner / D
    ).astype(BF16)
    return (moe_out, grad_tokens, grad_combine)


def solution(mesh):
    placed = (
        P("region", "local"),
        P("local"),
        P("region", None, "local"),
        P("region", None, "local"),
        P("region", "local", None),
        P("region", None),
        P("region", None),
        P("region", "local"),
    )
    return jax.shard_map(
        on_device,
        mesh=mesh,
        in_specs=placed,
        out_specs=(P("region", "local"), P("region", "local"), P("region", None)),
        check_vma=False,
    )
```

```python
import jax
import jax.numpy as jnp
from jax import lax
from jax.sharding import PartitionSpec as P

D = 7168
F32 = jnp.float32
BF16 = jnp.bfloat16
LAST = (((1,), (1,)), ((), ()))


def dot(left, right):
    return jnp.dot(left, right, preferred_element_type=F32)


def split_weights(weights):
    high = weights.astype(BF16)
    return high, (weights - high.astype(F32)).astype(BF16)


def on_device(tokens, norm_gain, w_gate, w_up, w_down, regions, combine, grad_out):
    token_count, width_local = tokens.shape
    region_count = lax.axis_size("region")
    route_count = regions.shape[1]
    capacity = max(2, token_count * route_count * 5 // (4 * region_count))
    slot_total = region_count * capacity
    gate_w, up_w, down_w = w_gate[0], w_up[0], w_down[0]

    share_count = lax.axis_size("local")

    def gather(matrix):
        return lax.all_gather(matrix, "local", axis=1, tiled=True)

    def stack_shares(matrix):
        width = matrix.shape[1] // share_count
        return jnp.stack([matrix[:, z * width:(z + 1) * width] for z in range(share_count)])

    def scatter(stacked):
        return lax.psum_scatter(stacked, "local", scatter_dimension=0, tiled=False)

    flat_routes = regions.reshape(-1)
    one_hot = (flat_routes[:, None] == jnp.arange(region_count, dtype=jnp.int32)[None, :]).astype(F32)
    pairs = token_count * route_count
    earlier = (jnp.arange(pairs)[:, None] > jnp.arange(pairs)[None, :]).astype(F32)
    running = dot(earlier.astype(BF16), one_hot.astype(BF16))
    slot_index = jnp.sum(running * one_hot, axis=1).astype(jnp.int32)
    placement = (flat_routes * capacity + slot_index).reshape(token_count, route_count)
    hits = placement[:, :, None] == jnp.arange(slot_total, dtype=jnp.int32)[None, None, :]
    spread = jnp.sum(hits.astype(F32), axis=1).astype(BF16)
    weighted = jnp.sum(jnp.where(hits, combine[:, :, None], 0.0), axis=1)
    weight_high, weight_low = split_weights(weighted)

    def pack_rows(matrix):
        picked = lax.dot_general(spread, matrix, (((0,), (0,)), ((), ())), preferred_element_type=F32)
        return picked.astype(BF16).reshape(region_count, capacity, matrix.shape[1])

    def exchange(blocks):
        return lax.all_to_all(blocks, "region", split_axis=0, concat_axis=0, tiled=True)

    far_blocks = exchange(pack_rows(grad_out)).reshape(slot_total, width_local)
    gain_high, gain_rest = split_weights(norm_gain)
    gain_mid, gain_low = split_weights(norm_gain - gain_high.astype(F32))
    gain_rows = jnp.stack([gain_high, gain_mid, gain_low])
    tokens_cat = jnp.concatenate([tokens, jnp.pad(gain_rows, ((0, 5), (0, 0)))], axis=0)
    tokens_full = gather(tokens_cat)
    far_blocks, tokens_full = lax.optimization_barrier((far_blocks, tokens_full))
    rows_grad = gather(far_blocks)

    gain_full = jnp.sum(tokens_full[token_count:token_count + 3].astype(F32), axis=0)
    inputs_full = tokens_full[:token_count].astype(F32)
    inv_rms = lax.rsqrt(jnp.sum(inputs_full * inputs_full, axis=1, keepdims=True) / D + 1e-06)
    normed = (inputs_full * inv_rms * gain_full).astype(BF16)
    rows_in = exchange(pack_rows(normed)).reshape(slot_total, D)
    gate_pre = dot(rows_in, gate_w)
    up_pre = dot(rows_in, up_w)
    sig_gate = jax.nn.sigmoid(gate_pre)
    act_gate = gate_pre * sig_gate
    hidden = (act_gate * up_pre).astype(BF16)
    expert_out = stack_shares(dot(hidden, down_w).astype(BF16))
    expert_out, rows_grad = lax.optimization_barrier((expert_out, rows_grad))
    grad_hidden = lax.dot_general(rows_grad, down_w, LAST, preferred_element_type=F32)
    grad_gate = (grad_hidden * up_pre * sig_gate * (1.0 + gate_pre * (1.0 - sig_gate))).astype(BF16)
    grad_up = (grad_hidden * act_gate).astype(BF16)
    branch_grad = (
        lax.dot_general(grad_gate, gate_w, LAST, preferred_element_type=F32)
        + lax.dot_general(grad_up, up_w, LAST, preferred_element_type=F32)
    ).astype(BF16)

    comb_part = jnp.sum(hidden.astype(F32) * grad_hidden, axis=1)
    inner_part = jnp.sum(grad_gate.astype(F32) * gate_pre + grad_up.astype(F32) * up_pre, axis=1)

    scalars = jnp.stack([comb_part, inner_part], axis=1)
    scalars = jnp.concatenate(split_weights(scalars), axis=1)
    scalars = jnp.pad(scalars, ((0, 0), (0, 124)))

    def send_home(rows):
        return exchange(rows.reshape(region_count, capacity, rows.shape[1])).reshape(slot_total, rows.shape[1])

    def combined(rows):
        return dot(weight_high, rows) + dot(weight_low, rows)

    out_share = scatter(expert_out)
    back_grad = send_home(jnp.concatenate([branch_grad, scalars], axis=1))
    picked = jnp.einsum("tks,sc->tkc", hits.astype(BF16), back_grad[:, D:], preferred_element_type=F32)
    picked = lax.psum(picked[:, :, :2] + picked[:, :, 2:4], "local")
    grad_combine = picked[:, :, 0]
    inner = jnp.sum(picked[:, :, 1] * combine, axis=1, keepdims=True) / inv_rms
    grad_sum = stack_shares(combined(back_grad[:, :D]).astype(BF16))
    grad_sum, out_share = lax.optimization_barrier((grad_sum, out_share))
    grad_normed = scatter(grad_sum)
    moe_out = combined(send_home(out_share)).astype(BF16)
    scaled = norm_gain * grad_normed.astype(F32)
    grad_tokens = (
        inv_rms * scaled - tokens.astype(F32) * inv_rms * inv_rms * inv_rms * inner / D
    ).astype(BF16)
    return (moe_out, grad_tokens, grad_combine)


def solution(mesh):
    placed = (
        P("region", "local"),
        P("local"),
        P("region", None, "local"),
        P("region", None, "local"),
        P("region", "local", None),
        P("region", None),
        P("region", None),
        P("region", "local"),
    )
    return jax.shard_map(
        on_device,
        mesh=mesh,
        in_specs=placed,
        out_specs=(P("region", "local"), P("region", "local"), P("region", None)),
        check_vma=False,
    )
```

```python
import jax
import jax.numpy as jnp
from jax import lax
from jax.sharding import PartitionSpec as P

D = 7168
F32 = jnp.float32
BF16 = jnp.bfloat16
LAST = (((1,), (1,)), ((), ()))


def dot(left, right):
    return jnp.dot(left, right, preferred_element_type=F32)


def split_weights(weights):
    high = weights.astype(BF16)
    return high, (weights - high.astype(F32)).astype(BF16)


def on_device(tokens, norm_gain, w_gate, w_up, w_down, regions, combine, grad_out):
    token_count, width_local = tokens.shape
    region_count = lax.axis_size("region")
    route_count = regions.shape[1]
    capacity = max(2, token_count * route_count * 5 // (4 * region_count))
    slot_total = region_count * capacity
    gate_w, up_w, down_w = w_gate[0], w_up[0], w_down[0]

    share_count = lax.axis_size("local")

    def gather(matrix):
        return lax.all_gather(matrix, "local", axis=1, tiled=True)

    def stack_shares(matrix):
        width = matrix.shape[1] // share_count
        return jnp.stack([matrix[:, z * width:(z + 1) * width] for z in range(share_count)])

    def scatter(stacked):
        return lax.psum_scatter(stacked, "local", scatter_dimension=0, tiled=False)

    flat_routes = regions.reshape(-1)
    one_hot = (flat_routes[:, None] == jnp.arange(region_count, dtype=jnp.int32)[None, :]).astype(F32)
    pairs = token_count * route_count
    earlier = (jnp.arange(pairs)[:, None] > jnp.arange(pairs)[None, :]).astype(F32)
    running = dot(earlier.astype(BF16), one_hot.astype(BF16))
    slot_index = jnp.sum(running * one_hot, axis=1).astype(jnp.int32)
    placement = (flat_routes * capacity + slot_index).reshape(token_count, route_count)
    hits = placement[:, :, None] == jnp.arange(slot_total, dtype=jnp.int32)[None, None, :]
    spread = jnp.sum(hits.astype(F32), axis=1).astype(BF16)
    weighted = jnp.sum(jnp.where(hits, combine[:, :, None], 0.0), axis=1)
    weight_high, weight_low = split_weights(weighted)

    def pack_rows(matrix):
        picked = lax.dot_general(spread, matrix, (((0,), (0,)), ((), ())), preferred_element_type=F32)
        return picked.astype(BF16).reshape(region_count, capacity, matrix.shape[1])

    def exchange(blocks):
        return lax.all_to_all(blocks, "region", split_axis=0, concat_axis=0, tiled=True)

    far_blocks = exchange(pack_rows(grad_out)).reshape(slot_total, width_local)
    gain_high, gain_rest = split_weights(norm_gain)
    gain_mid, gain_low = split_weights(norm_gain - gain_high.astype(F32))
    gain_rows = jnp.stack([gain_high, gain_mid, gain_low])
    tokens_cat = jnp.concatenate([tokens, jnp.pad(gain_rows, ((0, 5), (0, 0)))], axis=0)
    tokens_full = gather(tokens_cat)
    far_blocks, tokens_full = lax.optimization_barrier((far_blocks, tokens_full))
    rows_grad = gather(far_blocks)

    gain_full = jnp.sum(tokens_full[token_count:token_count + 3].astype(F32), axis=0)
    inputs_full = tokens_full[:token_count].astype(F32)
    inv_rms = lax.rsqrt(jnp.sum(inputs_full * inputs_full, axis=1, keepdims=True) / D + 1e-06)
    normed = (inputs_full * inv_rms * gain_full).astype(BF16)
    rows_in = exchange(pack_rows(normed)).reshape(slot_total, D)
    gate_pre = dot(rows_in, gate_w)
    up_pre = dot(rows_in, up_w)
    gate_pre, up_pre, rows_grad = lax.optimization_barrier((gate_pre, up_pre, rows_grad))
    sig_gate = jax.nn.sigmoid(gate_pre)
    act_gate = gate_pre * sig_gate
    hidden = (act_gate * up_pre).astype(BF16)
    expert_out = stack_shares(dot(hidden, down_w).astype(BF16))
    expert_out, rows_grad = lax.optimization_barrier((expert_out, rows_grad))
    grad_hidden = lax.dot_general(rows_grad, down_w, LAST, preferred_element_type=F32)
    grad_gate = (grad_hidden * up_pre * sig_gate * (1.0 + gate_pre * (1.0 - sig_gate))).astype(BF16)
    grad_up = (grad_hidden * act_gate).astype(BF16)
    branch_grad = (
        lax.dot_general(grad_gate, gate_w, LAST, preferred_element_type=F32)
        + lax.dot_general(grad_up, up_w, LAST, preferred_element_type=F32)
    ).astype(BF16)

    comb_part = jnp.sum(hidden.astype(F32) * grad_hidden, axis=1)
    inner_part = jnp.sum(grad_gate.astype(F32) * gate_pre + grad_up.astype(F32) * up_pre, axis=1)

    scalars = jnp.stack([comb_part, inner_part], axis=1)
    scalars = jnp.concatenate(split_weights(scalars), axis=1)
    scalars = jnp.pad(scalars, ((0, 0), (0, 124)))

    def send_home(rows):
        return exchange(rows.reshape(region_count, capacity, rows.shape[1])).reshape(slot_total, rows.shape[1])

    def combined(rows):
        return dot(weight_high, rows) + dot(weight_low, rows)

    out_share = scatter(expert_out)
    back_grad = send_home(jnp.concatenate([branch_grad, scalars], axis=1))
    picked = jnp.einsum("tks,sc->tkc", hits.astype(BF16), back_grad[:, D:], preferred_element_type=F32)
    picked = lax.psum(picked[:, :, :2] + picked[:, :, 2:4], "local")
    grad_combine = picked[:, :, 0]
    inner = jnp.sum(picked[:, :, 1] * combine, axis=1, keepdims=True) / inv_rms
    grad_sum = stack_shares(combined(back_grad[:, :D]).astype(BF16))
    grad_sum, out_share = lax.optimization_barrier((grad_sum, out_share))
    grad_normed = scatter(grad_sum)
    moe_out = combined(send_home(out_share)).astype(BF16)
    scaled = norm_gain * grad_normed.astype(F32)
    grad_tokens = (
        inv_rms * scaled - tokens.astype(F32) * inv_rms * inv_rms * inv_rms * inner / D
    ).astype(BF16)
    return (moe_out, grad_tokens, grad_combine)


def solution(mesh):
    placed = (
        P("region", "local"),
        P("local"),
        P("region", None, "local"),
        P("region", None, "local"),
        P("region", "local", None),
        P("region", None),
        P("region", None),
        P("region", "local"),
    )
    return jax.shard_map(
        on_device,
        mesh=mesh,
        in_specs=placed,
        out_specs=(P("region", "local"), P("region", "local"), P("region", None)),
        check_vma=False,
    )
```
